32 devices in a mesh: group: 2 (over y), wide: 4 (over z), narrow: 4 (over x, core).
Axes of the slice: x: 2, y: 2, z: 4, core: 2. Of those that a mesh axis runs over, the one named last changes fastest.
Arguments:
- field: bfloat16 [32768, 512], P(('group', 'wide', 'narrow')), parts along dimension 0, may hold values from -24 to 24
- w_embed: bfloat16 [512, 512], replicated, may hold values from -0.25 to 0.25
- embed_bias: float32 [512], replicated, may hold values from -4 to 4
- w_query: bfloat16 [512, 512], replicated, may hold values from -0.25 to 0.25
- w_key: bfloat16 [512, 512], replicated, may hold values from -0.25 to 0.25
- w_value: bfloat16 [512, 512], replicated, may hold values from -0.25 to 0.25
- w_out: bfloat16 [512, 512], replicated, may hold values from -0.25 to 0.25
- latents: bfloat16 [512, 512], replicated, may hold values from -120 to 120
- out_gain: float32 [512], replicated, may hold values from 0.5 to 1.5
Outputs:
- encoded: bfloat16 [1024, 512], P('group'), parts along dimension 0
The draws below stay inside these ranges and needn't reach their ends.
There are 2 independent parts, one for each index of `group`. The reference program is written for one: setup_inputs(seed, part) draws one part's arguments, and reference() takes and returns one part's arrays. A program takes and returns all parts, laid end to end along the dimension named above; an argument that names none is the same for every part. Nothing has to cross between parts.
All inputs are finite; a program needn't handle non-finite values.
Results may differ from the reference program's by a relative error of at most 0.012.
The reference program's roundings to bfloat16 on the way count: a program that leaves them out, or rounds other values in their place, can miss the bound.
Values may be sent and summed in bfloat16 or wider, within the bound.
A program may use at most 64 MiB of HBM per device.

```python
import jax
import jax.numpy as jnp
from jax import lax

PATCH = 512
D = 512
HEADS = 8
LATENTS = 512
TOK_DEV = 1024
TOKENS = 16384


def draw_field(key, part):
    key = jax.random.fold_in(key, 11)
    first, second, third = jax.random.split(key, 3)
    position = jnp.arange(TOKENS, dtype=jnp.float32)[:, None]
    rising = jnp.exp(jnp.log(3.0) * position / TOKENS)
    rough = jnp.exp(jax.random.uniform(second, (TOKENS, 1), minval=0.0, maxval=jnp.log(2.0)))
    base = jax.random.truncated_normal(first, -4.0, 4.0, (TOKENS, PATCH))
    common = jax.random.truncated_normal(third, -3.0, 3.0, (TOKENS // TOK_DEV, 1, PATCH)) * 5.0
    common = jnp.broadcast_to(common, (TOKENS // TOK_DEV, TOK_DEV, PATCH)).reshape(TOKENS, PATCH)
    total = jnp.clip(0.5 * base * rising * rough + common, -24.0, 24.0)
    return total.astype(jnp.bfloat16)


def draw_latents(key, part):
    key = jax.random.fold_in(key, 12)
    first = jax.random.fold_in(key, 0)
    base = jax.random.truncated_normal(first, -4.0, 4.0, (LATENTS, D)) * 0.5
    return base.astype(jnp.bfloat16)


def gaussian(stream_key, dims, scale, limit, kind=jnp.bfloat16):
    result = jax.random.normal(stream_key, dims, jnp.float32) * scale
    return jnp.minimum(jnp.maximum(result, -limit), limit).astype(kind)


def setup_inputs(seed: int = 0, part: int = 0) -> dict:
    streams_of = jax.random.split(jax.random.key(seed), 10)
    own_keys = jax.random.split(jax.random.fold_in(streams_of[9], part), 10)
    return {
        "field": draw_field(jax.random.fold_in(jax.random.fold_in(streams_of[9], part), 71), part),
        "w_embed": gaussian(streams_of[1], (PATCH, D), PATCH ** -0.5, 0.25),
        "embed_bias": gaussian(streams_of[2], (D,), 1.0, 4.0, jnp.float32),
        "w_query": gaussian(streams_of[3], (D, D), D ** -0.5, 0.25),
        "w_key": gaussian(streams_of[4], (D, D), D ** -0.5, 0.25),
        "w_value": gaussian(streams_of[5], (D, D), D ** -0.5, 0.25),
        "w_out": gaussian(streams_of[6], (D, D), D ** -0.5, 0.25),
        "latents": draw_latents(jax.random.fold_in(streams_of[9], 71), part),
        "out_gain": jnp.clip(1.0 + 0.1 * jax.random.normal(streams_of[8], (D,), jnp.float32), 0.5, 1.5),
    }


def reference(field, w_embed, embed_bias, w_query, w_key, w_value, w_out, latents, out_gain):
    head_dim = D // HEADS
    emb = (jnp.dot(field, w_embed, preferred_element_type=jnp.float32) + embed_bias).astype(jnp.bfloat16)
    keys = jnp.dot(emb, w_key, preferred_element_type=jnp.float32).astype(jnp.bfloat16)
    values = jnp.dot(emb, w_value, preferred_element_type=jnp.float32).astype(jnp.bfloat16)
    queries = (jnp.dot(latents, w_query, preferred_element_type=jnp.float32) * head_dim ** (-0.5)).astype(jnp.bfloat16)
    query_heads = queries.reshape(LATENTS, HEADS, head_dim).transpose(1, 0, 2)
    key_heads = keys.reshape(TOKENS, HEADS, head_dim).transpose(1, 0, 2)
    value_heads = values.reshape(TOKENS, HEADS, head_dim).transpose(1, 0, 2)

    def one_head(operands):
        query, key_part, value_part = operands
        scores = jnp.dot(query, key_part.T, preferred_element_type=jnp.float32)
        top = lax.optimization_barrier(jnp.max(scores, axis=1, keepdims=True))
        expo = jnp.exp(scores - top)
        denom = lax.optimization_barrier(jnp.sum(expo, axis=1))
        numer = jnp.dot(expo.astype(jnp.bfloat16), value_part, preferred_element_type=jnp.float32)
        return (numer, denom)
    numer, denom = lax.map(one_head, (query_heads, key_heads, value_heads))
    attended = (numer / denom[:, :, None]).transpose(1, 0, 2).reshape(LATENTS, D).astype(jnp.bfloat16)
    mixed = latents.astype(jnp.float32) + jnp.dot(attended, w_out, preferred_element_type=jnp.float32)
    center = mixed - lax.optimization_barrier(jnp.mean(mixed, axis=1, keepdims=True))
    spread = lax.optimization_barrier(jnp.mean(center * center, axis=1, keepdims=True))
    return (center * lax.rsqrt(spread + 1e-05) * out_gain).astype(jnp.bfloat16)
```

```python
import functools

import jax
import jax.numpy as jnp
from jax import lax
from jax.experimental import pallas as pl
from jax.experimental.pallas import tpu as pltpu
from jax.sharding import PartitionSpec as P

HEADS = 8
F32 = jnp.float32
BF16 = jnp.bfloat16
MESH = pl.DeviceIdType.MESH


def finish(numer, denom, latent_rows, w_out, out_gain, heads):
    count, width = numer.shape
    ratio = numer.reshape(count, heads, width // heads) / denom[:, :, None]
    attended = ratio.reshape(count, width).astype(BF16)
    mixed = latent_rows.astype(F32) + jnp.dot(attended, w_out, preferred_element_type=F32)
    center = mixed - jnp.mean(mixed, axis=1, keepdims=True)
    spread = jnp.mean(center * center, axis=1, keepdims=True)
    return (center * lax.rsqrt(spread + 1e-05) * out_gain).astype(BF16)


def plain_body(field, w_embed, embed_bias, w_query, w_key, w_value, w_out, latents, out_gain):
    tok_rows = field.shape[0]
    lat_rows, width = latents.shape
    heads = HEADS
    head_dim = width // heads
    emb = (jnp.dot(field, w_embed, preferred_element_type=F32) + embed_bias).astype(BF16)
    keys = jnp.dot(emb, w_key, preferred_element_type=F32).astype(BF16)
    values = jnp.dot(emb, w_value, preferred_element_type=F32).astype(BF16)
    queries = (jnp.dot(latents, w_query, preferred_element_type=F32) * head_dim ** (-0.5)).astype(
        BF16
    )
    query_heads = queries.reshape(lat_rows, heads, head_dim)
    key_heads = keys.reshape(tok_rows, heads, head_dim)
    value_heads = values.reshape(tok_rows, heads, head_dim)
    scores = jnp.einsum("lhe,the->hlt", query_heads, key_heads, preferred_element_type=F32)
    top = lax.pmax(jnp.max(scores, axis=2), ("wide", "narrow"))
    expo = jnp.exp(scores - top[:, :, None])
    denom = jnp.sum(expo, axis=2).T
    numer = jnp.einsum(
        "hlt,the->lhe", expo.astype(BF16), value_heads, preferred_element_type=F32
    ).reshape(lat_rows, width)
    numer, denom = lax.psum((numer, denom), ("wide", "narrow"))
    return finish(numer, denom, latents, w_out, out_gain, heads)


TOP_COLS = 24
STAT_COLS = 40


def lanes(shape):
    return lax.broadcasted_iota(jnp.int32, shape, len(shape) - 1)


def encode(stat):
    high = stat.astype(BF16).astype(F32)
    rest = stat - high
    middle = rest.astype(BF16).astype(F32)
    low = rest - middle
    group = lanes(stat.shape) // 8
    part = jnp.where((group == 0) | (group == 3), high, jnp.where(group == 2, low, middle))
    return part.astype(BF16)


def make_spread(spread, width, heads):
    head_dim = width // heads
    row = lax.broadcasted_iota(jnp.int32, (128, width), 0)
    col = lanes((128, width))
    same = (row % 8) == (col // head_dim)
    spread[:, :width] = jnp.where(same & (row < TOP_COLS), 1.0, 0.0).astype(BF16)
    denom = same & (row >= TOP_COLS) & (row < STAT_COLS)
    spread[:, width + 256 :] = jnp.where(denom, 1.0, 0.0).astype(BF16)
    row = lax.broadcasted_iota(jnp.int32, (128, 128), 0)
    col = lanes((128, 128))
    same = ((row % 8) == (col % 8)) & (col < STAT_COLS)
    spread[:, width : width + 128] = jnp.where(same & (row < TOP_COLS), 1.0, 0.0).astype(BF16)
    denom = same & (row >= TOP_COLS) & (row < STAT_COLS)
    spread[:, width + 128 : width + 256] = jnp.where(denom, 1.0, 0.0).astype(BF16)


def merge(numers, stats, spread, width):
    full = [jnp.dot(s, spread[:, : width + 256], preferred_element_type=F32) for s in stats]
    top = functools.reduce(jnp.maximum, [f[:, : width + 128] for f in full])
    scale = [jnp.exp(f[:, : width + 128] - top) for f in full]
    numer = sum(n.astype(F32) * s[:, :width] for n, s in zip(numers, scale))
    denom = sum(f[:, width + 128 :] * s[:, width:] for f, s in zip(full, scale))
    stat = jnp.where(lanes(denom.shape) < TOP_COLS, top[:, width:], denom)
    return numer, encode(stat)


def merge_ratio(numers, stats, spread, width):
    full = [jnp.dot(s, spread[...], preferred_element_type=F32) for s in stats]
    top = functools.reduce(jnp.maximum, [f[:, :width] for f in full])
    scale = [jnp.exp(f[:, :width] - top) for f in full]
    numer = sum(n.astype(F32) * s for n, s in zip(numers, scale))
    denom = sum(f[:, width + 256 :] * s for f, s in zip(full, scale))
    return numer / denom


def kernel(
    deep,
    field,
    w_embed,
    embed_bias,
    w_query,
    w_key,
    w_value,
    w_out,
    latents,
    out_gain,
    out,
    queries,
    keys_t,
    vaug,
    spread,
    own_numer,
    own_stat,
    core_out,
    core_in,
    x_out,
    x_in,
    z_out,
    z_in,
    send,
    recv,
):
    tokens = field.shape[0]
    rows, width = latents.shape
    heads = HEADS
    head_dim = width // heads
    half, quarter, piece = rows // 2, rows // 4, rows // 4 // deep

    group, w, n = lax.axis_index("group"), lax.axis_index("wide"), lax.axis_index("narrow")
    c, x = lax.rem(n, 2), n // 2
    sibling = (group, w, x * 2 + 1 - c)
    across = (group, w, (1 - x) * 2 + c)
    along = [None] + [(group, lax.rem(w + k, deep), n) for k in range(1, deep)]

    barrier = pltpu.get_barrier_semaphore()
    for other in [sibling, across] + along[1:]:
        pl.semaphore_signal(barrier, inc=1, device_id=other, device_id_type=MESH)

    def copy(index, source, target, device):
        return pltpu.make_async_remote_copy(
            src_ref=source,
            dst_ref=target,
            send_sem=send.at[index],
            recv_sem=recv.at[index],
            device_id=device,
            device_id_type=MESH,
        )

    make_spread(spread, width, heads)
    queries[...] = (
        jnp.dot(latents[...], w_query[...], preferred_element_type=F32) * head_dim ** (-0.5)
    ).astype(BF16)

    chunk = 256

    @pl.loop(0, tokens // chunk)
    def project(step):
        at = pl.multiple_of(step * chunk, chunk)
        emb = (
            jnp.dot(field[pl.ds(at, chunk), :], w_embed[...], preferred_element_type=F32)
            + embed_bias[...]
        ).astype(BF16)
        keys = jnp.dot(emb, w_key[...], preferred_element_type=F32).astype(BF16)
        keys_t[:, pl.ds(at, chunk)] = keys.T
        values = jnp.dot(emb, w_value[...], preferred_element_type=F32)
        lane = lanes((chunk, 128))
        for pair in range(heads // 2):
            both = values[:, pair * 128 : pair * 128 + 128]
            for side in range(2):
                mine = (lane // head_dim) == side
                ones = (lane % 8 == pair * 2 + side) & (lane >= TOP_COLS) & (lane < STAT_COLS)
                target = pl.ds(side * tokens + at, chunk)
                vaug[pair, target, :128] = jnp.where(mine, both, 0.0).astype(BF16)
                vaug[pair, target, 128:] = jnp.where(ones, 1.0, 0.0).astype(BF16)

    def attend(start, numer_out, stat_out):
        lane = lanes((half, 128))
        stat = jnp.zeros((half, 128), F32)
        for pair in range(heads // 2):
            cols = slice(pair * 128, pair * 128 + 128)
            query = queries[pl.ds(start, half), cols]
            probs = []
            for side in range(2):
                one = jnp.where((lane // head_dim) == side, query.astype(F32), 0.0).astype(BF16)
                scores = jnp.dot(one, keys_t[cols, :], preferred_element_type=F32)
                top = jnp.max(scores, axis=1, keepdims=True)
                probs.append(jnp.exp(scores - top).astype(BF16))
                here = (lane % 8 == pair * 2 + side) & (lane < TOP_COLS)
                stat = jnp.where(here, top, stat)
            result = jnp.dot(
                jnp.concatenate(probs, axis=1), vaug[pair], preferred_element_type=F32
            )
            numer_out[:, cols] = result[:, :128].astype(numer_out.dtype)
            stat = stat + result[:, 128:]
        stat_out[...] = encode(stat)

    attend(
        pl.multiple_of((1 - c) * half, half), core_out.at[:, :width], core_out.at[:, width:]
    )
    pl.semaphore_wait(barrier, 1 + deep)
    sent = [copy(0, core_out, core_in, sibling)]
    sent[0].start()
    attend(pl.multiple_of(c * half, half), own_numer, own_stat)
    sent[0].wait_recv()

    def chip_sum(at):
        at = pl.multiple_of(at, piece)
        return merge(
            [own_numer[pl.ds(at, piece), :], core_in[pl.ds(at, piece), :width]],
            [own_stat[pl.ds(at, piece), :], core_in[pl.ds(at, piece), width:]],
            spread,
            width,
        )

    order = list(range(1, deep)) + [0]
    index = 1
    x_copies = {}
    for k in order:
        block = lax.rem(w + k, deep)
        numer, stat = chip_sum((1 - x) * quarter + block * piece)
        x_out[k, :, :width] = numer.astype(BF16)
        x_out[k, :, width:] = stat
        x_copies[k] = copy(index, x_out.at[k], x_in.at[k], across)
        x_copies[k].start()
        index += 1
    mine = {}
    for k in order:
        block = lax.rem(w + k, deep)
        mine[k] = chip_sum(x * quarter + block * piece)
    z_copies = {}
    for k in order:
        x_copies[k].wait_recv()
        numer, stat = merge(
            [mine[k][0], x_in[k, :, :width]], [mine[k][1], x_in[k, :, width:]], spread, width
        )
        if k:
            z_out[k, :, :width] = numer.astype(BF16)
            z_out[k, :, width:] = stat
            z_copies[k] = copy(index, z_out.at[k], z_in.at[k], along[k])
            z_copies[k].start()
            index += 1
    numers, stats = [numer], [stat]
    for k in order[:-1]:
        z_copies[k].wait_recv()
        numers.append(z_in[k, :, :width])
        stats.append(z_in[k, :, width:])
    attended = merge_ratio(numers, stats, spread, width).astype(BF16)

    def place(core, column, slab):
        return pl.ds(pl.multiple_of(core * half + column * quarter + slab * piece, piece), piece)

    own = place(c, x, w)
    mixed = latents[own, :].astype(F32) + jnp.dot(
        attended, w_out[...], preferred_element_type=F32
    )
    center = mixed - jnp.mean(mixed, axis=1, keepdims=True)
    variance = jnp.mean(center * center, axis=1, keepdims=True)
    out[own, :] = (center * lax.rsqrt(variance + 1e-05) * out_gain[...]).astype(BF16)

    z_gather, x_gather, s_gather = {}, {}, {}

    def gather(store, key, at, device):
        nonlocal index
        store[key] = copy(index, out.at[at], out.at[at], device)
        store[key].start()
        index += 1

    for k in range(1, deep):
        gather(z_gather, k, own, along[k])
    gather(x_gather, 0, own, across)
    gather(s_gather, 0, own, sibling)
    for k in range(1, deep):
        z_gather[k].wait_recv()
        came = place(c, x, lax.rem(w + deep - k, deep))
        gather(x_gather, k, came, across)
        gather(s_gather, k, came, sibling)
    for k in range(deep):
        x_gather[k].wait_recv()
        came = place(c, 1 - x, lax.rem(w + deep - k, deep))
        gather(s_gather, deep + k, came, sibling)
    for k in range(2 * deep):
        s_gather[k].wait_recv()
    for store in (x_copies, z_copies, z_gather, x_gather, s_gather):
        sent += list(store.values())
    for one in sent:
        one.wait_send()


def body(deep, field, w_embed, embed_bias, w_query, w_key, w_value, w_out, latents, out_gain):
    tokens = field.shape[0]
    rows, width = latents.shape
    half, piece = rows // 2, rows // 4 // deep
    wide = width + 128
    copies = 1 + deep + (deep - 1) + (deep - 1) + deep + 2 * deep
    macs = tokens * width * width * 3 + rows * width * width + 2 * rows * tokens * width
    return pl.pallas_call(
        functools.partial(kernel, deep),
        out_shape=jax.ShapeDtypeStruct((rows, width), BF16),
        in_specs=[pl.BlockSpec(memory_space=pltpu.VMEM)] * 9,
        out_specs=pl.BlockSpec(memory_space=pltpu.VMEM),
        scratch_shapes=[
            pltpu.VMEM((rows, width), BF16),
            pltpu.VMEM((width, tokens), BF16),
            pltpu.VMEM((HEADS // 2, 2 * tokens, 256), BF16),
            pltpu.VMEM((128, 2 * width + 256), BF16),
            pltpu.VMEM((half, width), F32),
            pltpu.VMEM((half, 128), BF16),
            pltpu.VMEM((half, wide), BF16),
            pltpu.VMEM((half, wide), BF16),
            pltpu.VMEM((deep, piece, wide), BF16),
            pltpu.VMEM((deep, piece, wide), BF16),
            pltpu.VMEM((deep, piece, wide), BF16),
            pltpu.VMEM((deep, piece, wide), BF16),
            pltpu.SemaphoreType.DMA((copies,)),
            pltpu.SemaphoreType.DMA((copies,)),
        ],
        compiler_params=pltpu.CompilerParams(
            collective_id=0, has_side_effects=True, vmem_limit_bytes=48 * 2**20
        ),
        cost_estimate=pl.CostEstimate(
            flops=2 * macs, bytes_accessed=5 * 2**20, transcendentals=rows * tokens * HEADS
        ),
    )(
        field,
        w_embed,
        embed_bias.reshape(1, width),
        w_query,
        w_key,
        w_value,
        w_out,
        latents,
        out_gain.reshape(1, width),
    )


def solution(mesh):
    placed = (P(("group", "wide", "narrow"), None), P(), P(), P(), P(), P(), P(), P(), P())
    deep = mesh.shape["wide"]

    def pick(field, *rest):
        rows, width = rest[6].shape
        fits = mesh.shape["narrow"] == 4 and 2 <= deep <= 8 and rows % (64 * deep) == 0
        fits = fits and width == HEADS * 64 and field.shape[0] % 256 == 0
        return (functools.partial(body, deep) if fits else plain_body)(field, *rest)

    return jax.shard_map(
        pick, mesh=mesh, in_specs=placed, out_specs=P("group", None), check_vma=False
    )
```

```python
import functools

import jax
import jax.numpy as jnp
from jax import lax
from jax.experimental import pallas as pl
from jax.experimental.pallas import tpu as pltpu
from jax.sharding import PartitionSpec as P

HEADS = 8
F32 = jnp.float32
BF16 = jnp.bfloat16
MESH = pl.DeviceIdType.MESH


def finish(numer, denom, latent_rows, w_out, out_gain, heads):
    count, width = numer.shape
    ratio = numer.reshape(count, heads, width // heads) / denom[:, :, None]
    attended = ratio.reshape(count, width).astype(BF16)
    mixed = latent_rows.astype(F32) + jnp.dot(attended, w_out, preferred_element_type=F32)
    center = mixed - jnp.mean(mixed, axis=1, keepdims=True)
    spread = jnp.mean(center * center, axis=1, keepdims=True)
    return (center * lax.rsqrt(spread + 1e-05) * out_gain).astype(BF16)


def plain_body(field, w_embed, embed_bias, w_query, w_key, w_value, w_out, latents, out_gain):
    tok_rows = field.shape[0]
    lat_rows, width = latents.shape
    heads = HEADS
    head_dim = width // heads
    emb = (jnp.dot(field, w_embed, preferred_element_type=F32) + embed_bias).astype(BF16)
    keys = jnp.dot(emb, w_key, preferred_element_type=F32).astype(BF16)
    values = jnp.dot(emb, w_value, preferred_element_type=F32).astype(BF16)
    queries = (jnp.dot(latents, w_query, preferred_element_type=F32) * head_dim ** (-0.5)).astype(
        BF16
    )
    query_heads = queries.reshape(lat_rows, heads, head_dim)
    key_heads = keys.reshape(tok_rows, heads, head_dim)
    value_heads = values.reshape(tok_rows, heads, head_dim)
    scores = jnp.einsum("lhe,the->hlt", query_heads, key_heads, preferred_element_type=F32)
    top = lax.pmax(jnp.max(scores, axis=2), ("wide", "narrow"))
    expo = jnp.exp(scores - top[:, :, None])
    denom = jnp.sum(expo, axis=2).T
    numer = jnp.einsum(
        "hlt,the->lhe", expo.astype(BF16), value_heads, preferred_element_type=F32
    ).reshape(lat_rows, width)
    numer, denom = lax.psum((numer, denom), ("wide", "narrow"))
    return finish(numer, denom, latents, w_out, out_gain, heads)


TOP_COLS = 24
STAT_COLS = 40


def lanes(shape):
    return lax.broadcasted_iota(jnp.int32, shape, len(shape) - 1)


def encode(stat):
    high = stat.astype(BF16).astype(F32)
    rest = stat - high
    middle = rest.astype(BF16).astype(F32)
    low = rest - middle
    group = lanes(stat.shape) // 8
    part = jnp.where((group == 0) | (group == 3), high, jnp.where(group == 2, low, middle))
    return part.astype(BF16)


def make_spread(spread, width, heads):
    head_dim = width // heads
    row = lax.broadcasted_iota(jnp.int32, (128, width), 0)
    col = lanes((128, width))
    same = (row % 8) == (col // head_dim)
    spread[:, :width] = jnp.where(same & (row < TOP_COLS), 1.0, 0.0).astype(BF16)
    denom = same & (row >= TOP_COLS) & (row < STAT_COLS)
    spread[:, width + 256 :] = jnp.where(denom, 1.0, 0.0).astype(BF16)
    row = lax.broadcasted_iota(jnp.int32, (128, 128), 0)
    col = lanes((128, 128))
    same = ((row % 8) == (col % 8)) & (col < STAT_COLS)
    spread[:, width : width + 128] = jnp.where(same & (row < TOP_COLS), 1.0, 0.0).astype(BF16)
    denom = same & (row >= TOP_COLS) & (row < STAT_COLS)
    spread[:, width + 128 : width + 256] = jnp.where(denom, 1.0, 0.0).astype(BF16)


def merge(numers, stats, spread, width):
    full = [jnp.dot(s, spread[:, : width + 256], preferred_element_type=F32) for s in stats]
    top = functools.reduce(jnp.maximum, [f[:, : width + 128] for f in full])
    scale = [jnp.exp(f[:, : width + 128] - top) for f in full]
    numer = sum(n.astype(F32) * s[:, :width] for n, s in zip(numers, scale))
    denom = sum(f[:, width + 128 :] * s[:, width:] for f, s in zip(full, scale))
    stat = jnp.where(lanes(denom.shape) < TOP_COLS, top[:, width:], denom)
    return numer, encode(stat)


def merge_ratio(numers, stats, spread, width):
    full = [jnp.dot(s, spread[...], preferred_element_type=F32) for s in stats]
    top = functools.reduce(jnp.maximum, [f[:, :width] for f in full])
    scale = [jnp.exp(f[:, :width] - top) for f in full]
    numer = sum(n.astype(F32) * s for n, s in zip(numers, scale))
    denom = sum(f[:, width + 256 :] * s for f, s in zip(full, scale))
    return numer / denom


def kernel(
    deep,
    *refs,
):
    sources, out, held = refs[:9], refs[9], refs[10:19]
    field, w_embed, embed_bias, w_query, w_key, w_value, w_out, latents, out_gain = held
    load = refs[-1]
    compute(deep, Loads(sources, held, load), *held, out, *refs[19:-1])


class Loads:
    ORDER = (7, 3, 0, 1, 2, 4, 5, 6, 8)

    def __init__(self, sources, held, load):
        self.copies = [
            pltpu.make_async_copy(source, target, load.at[i])
            for i, (source, target) in enumerate(zip(sources, held))
        ]

    def start(self):
        for i in self.ORDER:
            self.copies[i].start()

    def wait(self, *which):
        for i in which:
            self.copies[i].wait()


def compute(
    deep,
    loads,
    field,
    w_embed,
    embed_bias,
    w_query,
    w_key,
    w_value,
    w_out,
    latents,
    out_gain,
    out,
    queries,
    keys_t,
    vaug,
    spread,
    own_numer,
    own_stat,
    core_out,
    core_in,
    x_out,
    x_in,
    z_out,
    z_in,
    mine_numer,
    mine_stat,
    send,
    recv,
):
    tokens = field.shape[0]
    rows, width = latents.shape
    heads = HEADS
    head_dim = width // heads
    half, quarter, piece = rows // 2, rows // 4, rows // 4 // deep

    loads.start()
    group, w, n = lax.axis_index("group"), lax.axis_index("wide"), lax.axis_index("narrow")
    c, x = lax.rem(n, 2), n // 2
    sibling = (group, w, x * 2 + 1 - c)
    across = (group, w, (1 - x) * 2 + c)
    along = [None] + [(group, lax.rem(w + k, deep), n) for k in range(1, deep)]

    barrier = pltpu.get_barrier_semaphore()
    for other in [sibling, across] + along[1:]:
        pl.semaphore_signal(barrier, inc=1, device_id=other, device_id_type=MESH)

    def copy(index, source, target, device):
        return pltpu.make_async_remote_copy(
            src_ref=source,
            dst_ref=target,
            send_sem=send.at[index],
            recv_sem=recv.at[index],
            device_id=device,
            device_id_type=MESH,
        )

    make_spread(spread, width, heads)
    loads.wait(3, 7)
    queries[...] = (
        jnp.dot(latents[...], w_query[...], preferred_element_type=F32) * head_dim ** (-0.5)
    ).astype(BF16)

    chunk = 256
    loads.wait(0, 1, 2, 4, 5)

    @pl.loop(0, tokens // chunk)
    def project(step):
        at = pl.multiple_of(step * chunk, chunk)
        emb = (
            jnp.dot(field[pl.ds(at, chunk), :], w_embed[...], preferred_element_type=F32)
            + embed_bias[...]
        ).astype(BF16)
        keys = jnp.dot(emb, w_key[...], preferred_element_type=F32).astype(BF16)
        keys_t[:, pl.ds(at, chunk)] = keys.T
        values = jnp.dot(emb, w_value[...], preferred_element_type=F32)
        lane = lanes((chunk, 128))
        for pair in range(heads // 2):
            both = values[:, pair * 128 : pair * 128 + 128]
            for side in range(2):
                mine = (lane // head_dim) == side
                ones = (lane % 8 == pair * 2 + side) & (lane >= TOP_COLS) & (lane < STAT_COLS)
                target = pl.ds(side * tokens + at, chunk)
                vaug[pair, target, :128] = jnp.where(mine, both, 0.0).astype(BF16)
                vaug[pair, target, 128:] = jnp.where(ones, 1.0, 0.0).astype(BF16)

    def attend(start, numer_out, stat_out):
        lane = lanes((half, 128))
        stat = jnp.zeros((half, 128), F32)
        for pair in range(heads // 2):
            cols = slice(pair * 128, pair * 128 + 128)
            query = queries[pl.ds(start, half), cols]
            probs = []
            for side in range(2):
                one = jnp.where((lane // head_dim) == side, query.astype(F32), 0.0).astype(BF16)
                scores = jnp.dot(one, keys_t[cols, :], preferred_element_type=F32)
                top = jnp.max(scores, axis=1, keepdims=True)
                probs.append(jnp.exp(scores - top).astype(BF16))
                here = (lane % 8 == pair * 2 + side) & (lane < TOP_COLS)
                stat = jnp.where(here, top, stat)
            result = jnp.dot(
                jnp.concatenate(probs, axis=1), vaug[pair], preferred_element_type=F32
            )
            numer_out[:, cols] = result[:, :128].astype(numer_out.dtype)
            stat = stat + result[:, 128:]
        stat_out[...] = encode(stat)

    attend(
        pl.multiple_of((1 - c) * half, half), core_out.at[:, :width], core_out.at[:, width:]
    )
    pl.semaphore_wait(barrier, 1 + deep)
    sent = [copy(0, core_out, core_in, sibling)]
    sent[0].start()
    attend(pl.multiple_of(c * half, half), own_numer, own_stat)
    sent[0].wait_recv()

    def chip_sum(at):
        at = pl.multiple_of(at, quarter)
        return merge(
            [own_numer[pl.ds(at, quarter), :], core_in[pl.ds(at, quarter), :width]],
            [own_stat[pl.ds(at, quarter), :], core_in[pl.ds(at, quarter), width:]],
            spread,
            width,
        )

    order = list(range(1, deep)) + [0]
    index = 1
    x_copies = {}
    x_numer, x_stat = chip_sum((1 - x) * quarter)
    x_out[:, :width] = x_numer.astype(BF16)
    x_out[:, width:] = x_stat
    for k in order:
        block = pl.ds(pl.multiple_of(lax.rem(w + k, deep) * piece, piece), piece)
        x_copies[k] = copy(index, x_out.at[block], x_in.at[k], across)
        x_copies[k].start()
        index += 1
    x_numer, x_stat = chip_sum(x * quarter)
    mine_numer[...] = x_numer
    mine_stat[...] = x_stat
    mine = {}
    for k in order:
        block = pl.ds(pl.multiple_of(lax.rem(w + k, deep) * piece, piece), piece)
        mine[k] = (mine_numer[block, :], mine_stat[block, :])
    z_copies = {}
    for k in order:
        x_copies[k].wait_recv()
        numer, stat = merge(
            [mine[k][0], x_in[k, :, :width]], [mine[k][1], x_in[k, :, width:]], spread, width
        )
        if k:
            z_out[k, :, :width] = numer.astype(BF16)
            z_out[k, :, width:] = stat
            z_copies[k] = copy(index, z_out.at[k], z_in.at[k], along[k])
            z_copies[k].start()
            index += 1
    numers, stats = [numer], [stat]
    for k in order[:-1]:
        z_copies[k].wait_recv()
        numers.append(z_in[k, :, :width])
        stats.append(z_in[k, :, width:])
    attended = merge_ratio(numers, stats, spread, width).astype(BF16)

    def place(core, column, slab):
        return pl.ds(pl.multiple_of(core * half + column * quarter + slab * piece, piece), piece)

    own = place(c, x, w)
    loads.wait(6, 8)
    mixed = latents[own, :].astype(F32) + jnp.dot(
        attended, w_out[...], preferred_element_type=F32
    )
    center = mixed - jnp.mean(mixed, axis=1, keepdims=True)
    variance = jnp.mean(center * center, axis=1, keepdims=True)
    out[own, :] = (center * lax.rsqrt(variance + 1e-05) * out_gain[...]).astype(BF16)

    z_gather, x_gather, s_gather = {}, {}, {}

    def gather(store, key, at, device):
        nonlocal index
        store[key] = copy(index, out.at[at], out.at[at], device)
        store[key].start()
        index += 1

    for k in range(1, deep):
        gather(z_gather, k, own, along[k])
    gather(x_gather, 0, own, across)
    gather(s_gather, 0, own, sibling)

    def relay(k):
        x_gather[k].wait_recv()
        gather(s_gather, deep + k, place(c, 1 - x, lax.rem(w + deep - k, deep)), sibling)

    for k in range(1, deep):
        z_gather[k].wait_recv()
        came = place(c, x, lax.rem(w + deep - k, deep))
        gather(x_gather, k, came, across)
        gather(s_gather, k, came, sibling)
        if k > 1:
            relay(k - 2)
    relay(deep - 2)
    relay(deep - 1)
    for k in range(2 * deep):
        s_gather[k].wait_recv()
    for store in (x_copies, z_copies, z_gather, x_gather, s_gather):
        sent += list(store.values())
    for one in sent:
        one.wait_send()


def body(deep, field, w_embed, embed_bias, w_query, w_key, w_value, w_out, latents, out_gain):
    tokens = field.shape[0]
    rows, width = latents.shape
    half, piece = rows // 2, rows // 4 // deep
    wide = width + 128
    arguments = (
        field,
        w_embed,
        embed_bias.reshape(1, width),
        w_query,
        w_key,
        w_value,
        w_out,
        latents,
        out_gain.reshape(1, width),
    )
    copies = 1 + deep + (deep - 1) + (deep - 1) + deep + 2 * deep
    macs = tokens * width * width * 3 + rows * width * width + 2 * rows * tokens * width
    return pl.pallas_call(
        functools.partial(kernel, deep),
        out_shape=jax.ShapeDtypeStruct((rows, width), BF16),
        in_specs=[pl.BlockSpec(memory_space=pltpu.HBM)] * 9,
        out_specs=pl.BlockSpec(memory_space=pltpu.VMEM),
        scratch_shapes=[pltpu.VMEM(a.shape, a.dtype) for a in arguments]
        + [
            pltpu.VMEM((rows, width), BF16),
            pltpu.VMEM((width, tokens), BF16),
            pltpu.VMEM((HEADS // 2, 2 * tokens, 256), BF16),
            pltpu.VMEM((128, 2 * width + 256), BF16),
            pltpu.VMEM((half, width), F32),
            pltpu.VMEM((half, 128), BF16),
            pltpu.VMEM((half, wide), BF16),
            pltpu.VMEM((half, wide), BF16),
            pltpu.VMEM((rows // 4, wide), BF16),
            pltpu.VMEM((deep, piece, wide), BF16),
            pltpu.VMEM((deep, piece, wide), BF16),
            pltpu.VMEM((deep, piece, wide), BF16),
            pltpu.VMEM((rows // 4, width), F32),
            pltpu.VMEM((rows // 4, 128), BF16),
            pltpu.SemaphoreType.DMA((copies,)),
            pltpu.SemaphoreType.DMA((copies,)),
            pltpu.SemaphoreType.DMA((9,)),
        ],
        compiler_params=pltpu.CompilerParams(
            collective_id=0, has_side_effects=True, vmem_limit_bytes=63 * 2**20
        ),
        cost_estimate=pl.CostEstimate(
            flops=2 * macs, bytes_accessed=5 * 2**20, transcendentals=rows * tokens * HEADS
        ),
    )(*arguments)


def solution(mesh):
    placed = (P(("group", "wide", "narrow"), None), P(), P(), P(), P(), P(), P(), P(), P())
    deep = mesh.shape["wide"]

    def pick(field, *rest):
        rows, width = rest[6].shape
        fits = mesh.shape["narrow"] == 4 and 2 <= deep <= 8 and rows % (64 * deep) == 0
        fits = fits and width == HEADS * 64 and field.shape[0] % 256 == 0
        return (functools.partial(body, deep) if fits else plain_body)(field, *rest)

    return jax.shard_map(
        pick, mesh=mesh, in_specs=placed, out_specs=P("group", None), check_vma=False
    )
```

```python
import functools

import jax
import jax.numpy as jnp
from jax import lax
from jax.experimental import pallas as pl
from jax.experimental.pallas import tpu as pltpu
from jax.sharding import PartitionSpec as P

HEADS = 8
F32 = jnp.float32
BF16 = jnp.bfloat16
MESH = pl.DeviceIdType.MESH


def finish(numer, denom, latent_rows, w_out, out_gain, heads):
    count, width = numer.shape
    ratio = numer.reshape(count, heads, width // heads) / denom[:, :, None]
    attended = ratio.reshape(count, width).astype(BF16)
    mixed = latent_rows.astype(F32) + jnp.dot(attended, w_out, preferred_element_type=F32)
    center = mixed - jnp.mean(mixed, axis=1, keepdims=True)
    spread = jnp.mean(center * center, axis=1, keepdims=True)
    return (center * lax.rsqrt(spread + 1e-05) * out_gain).astype(BF16)


def plain_body(field, w_embed, embed_bias, w_query, w_key, w_value, w_out, latents, out_gain):
    tok_rows = field.shape[0]
    lat_rows, width = latents.shape
    heads = HEADS
    head_dim = width // heads
    emb = (jnp.dot(field, w_embed, preferred_element_type=F32) + embed_bias).astype(BF16)
    keys = jnp.dot(emb, w_key, preferred_element_type=F32).astype(BF16)
    values = jnp.dot(emb, w_value, preferred_element_type=F32).astype(BF16)
    queries = (jnp.dot(latents, w_query, preferred_element_type=F32) * head_dim ** (-0.5)).astype(
        BF16
    )
    query_heads = queries.reshape(lat_rows, heads, head_dim)
    key_heads = keys.reshape(tok_rows, heads, head_dim)
    value_heads = values.reshape(tok_rows, heads, head_dim)
    scores = jnp.einsum("lhe,the->hlt", query_heads, key_heads, preferred_element_type=F32)
    top = lax.pmax(jnp.max(scores, axis=2), ("wide", "narrow"))
    expo = jnp.exp(scores - top[:, :, None])
    denom = jnp.sum(expo, axis=2).T
    numer = jnp.einsum(
        "hlt,the->lhe", expo.astype(BF16), value_heads, preferred_element_type=F32
    ).reshape(lat_rows, width)
    numer, denom = lax.psum((numer, denom), ("wide", "narrow"))
    return finish(numer, denom, latents, w_out, out_gain, heads)


TOP_COLS = 24
STAT_COLS = 40


def lanes(shape):
    return lax.broadcasted_iota(jnp.int32, shape, len(shape) - 1)


def encode(stat):
    high = stat.astype(BF16).astype(F32)
    rest = stat - high
    middle = rest.astype(BF16).astype(F32)
    low = rest - middle
    group = lanes(stat.shape) // 8
    part = jnp.where((group == 0) | (group == 3), high, jnp.where(group == 2, low, middle))
    return part.astype(BF16)


def make_spread(spread, width, heads):
    head_dim = width // heads
    row = lax.broadcasted_iota(jnp.int32, (128, width), 0)
    col = lanes((128, width))
    same = (row % 8) == (col // head_dim)
    spread[:, :width] = jnp.where(same & (row < TOP_COLS), 1.0, 0.0).astype(BF16)
    denom = same & (row >= TOP_COLS) & (row < STAT_COLS)
    spread[:, width + 256 :] = jnp.where(denom, 1.0, 0.0).astype(BF16)
    row = lax.broadcasted_iota(jnp.int32, (128, 128), 0)
    col = lanes((128, 128))
    same = ((row % 8) == (col % 8)) & (col < STAT_COLS)
    spread[:, width : width + 128] = jnp.where(same & (row < TOP_COLS), 1.0, 0.0).astype(BF16)
    denom = same & (row >= TOP_COLS) & (row < STAT_COLS)
    spread[:, width + 128 : width + 256] = jnp.where(denom, 1.0, 0.0).astype(BF16)


def merge(numers, stats, spread, width):
    full = [jnp.dot(s, spread[:, : width + 256], preferred_element_type=F32) for s in stats]
    top = functools.reduce(jnp.maximum, [f[:, : width + 128] for f in full])
    scale = [jnp.exp(f[:, : width + 128] - top) for f in full]
    numer = sum(n.astype(F32) * s[:, :width] for n, s in zip(numers, scale))
    denom = sum(f[:, width + 128 :] * s[:, width:] for f, s in zip(full, scale))
    stat = jnp.where(lanes(denom.shape) < TOP_COLS, top[:, width:], denom)
    return numer, encode(stat)


def merge_ratio(numers, stats, spread, width):
    full = [jnp.dot(s, spread[...], preferred_element_type=F32) for s in stats]
    top = functools.reduce(jnp.maximum, [f[:, :width] for f in full])
    scale = [jnp.exp(f[:, :width] - top) for f in full]
    numer = sum(n.astype(F32) * s for n, s in zip(numers, scale))
    denom = sum(f[:, width + 256 :] * s for f, s in zip(full, scale))
    return numer / denom


def kernel(
    deep,
    *refs,
):
    sources, out, held = refs[:9], refs[9], refs[10:19]
    field, w_embed, embed_bias, w_query, w_key, w_value, w_out, latents, out_gain = held
    load = refs[-1]
    compute(deep, Loads(sources, held, load), *held, out, *refs[19:-1])


class Loads:
    ORDER = (7, 3, 0, 1, 2, 4, 5, 6, 8)

    def __init__(self, sources, held, load):
        self.copies = [
            pltpu.make_async_copy(source, target, load.at[i])
            for i, (source, target) in enumerate(zip(sources, held))
        ]

    def start(self):
        for i in self.ORDER:
            self.copies[i].start()

    def wait(self, *which):
        for i in which:
            self.copies[i].wait()


def compute(
    deep,
    loads,
    field,
    w_embed,
    embed_bias,
    w_query,
    w_key,
    w_value,
    w_out,
    latents,
    out_gain,
    out,
    queries,
    keys_t,
    vaug,
    spread,
    own_numer,
    own_stat,
    core_out,
    core_in,
    x_out,
    x_in,
    z_out,
    z_in,
    mine_numer,
    mine_stat,
    send,
    recv,
):
    tokens = field.shape[0]
    rows, width = latents.shape
    heads = HEADS
    head_dim = width // heads
    half, quarter, piece = rows // 2, rows // 4, rows // 4 // deep

    loads.start()
    group, w, n = lax.axis_index("group"), lax.axis_index("wide"), lax.axis_index("narrow")
    c, x = lax.rem(n, 2), n // 2
    sibling = (group, w, x * 2 + 1 - c)
    across = (group, w, (1 - x) * 2 + c)
    along = [None] + [(group, lax.rem(w + k, deep), n) for k in range(1, deep)]

    barrier = pltpu.get_barrier_semaphore()
    for other in [sibling, across] + along[1:]:
        pl.semaphore_signal(barrier, inc=1, device_id=other, device_id_type=MESH)

    def copy(index, source, target, device):
        return pltpu.make_async_remote_copy(
            src_ref=source,
            dst_ref=target,
            send_sem=send.at[index],
            recv_sem=recv.at[index],
            device_id=device,
            device_id_type=MESH,
        )

    make_spread(spread, width, heads)
    loads.wait(3, 7)
    queries[...] = (
        jnp.dot(latents[...], w_query[...], preferred_element_type=F32) * head_dim ** (-0.5)
    ).astype(BF16)

    chunk = 256
    loads.wait(0, 1, 2, 4, 5)

    @pl.loop(0, tokens // chunk)
    def project(step):
        at = pl.multiple_of(step * chunk, chunk)
        emb = (
            jnp.dot(field[pl.ds(at, chunk), :], w_embed[...], preferred_element_type=F32)
            + embed_bias[...]
        ).astype(BF16)
        keys = jnp.dot(emb, w_key[...], preferred_element_type=F32).astype(BF16)
        keys_t[:, pl.ds(at, chunk)] = keys.T
        values = jnp.dot(emb, w_value[...], preferred_element_type=F32)
        lane = lanes((chunk, 128))
        for pair in range(heads // 2):
            both = values[:, pair * 128 : pair * 128 + 128]
            for side in range(2):
                mine = (lane // head_dim) == side
                ones = (lane % 8 == pair * 2 + side) & (lane >= TOP_COLS) & (lane < STAT_COLS)
                target = pl.ds(side * tokens + at, chunk)
                vaug[pair, target, :128] = jnp.where(mine, both, 0.0).astype(BF16)
                vaug[pair, target, 128:] = jnp.where(ones, 1.0, 0.0).astype(BF16)

    def attend(start, numer_out, stat_out):
        lane = lanes((half, 128))
        stat = jnp.zeros((half, 128), F32)
        for pair in range(heads // 2):
            cols = slice(pair * 128, pair * 128 + 128)
            query = queries[pl.ds(start, half), cols]
            probs = []
            for side in range(2):
                one = jnp.where((lane // head_dim) == side, query.astype(F32), 0.0).astype(BF16)
                scores = jnp.dot(one, keys_t[cols, :], preferred_element_type=F32)
                top = jnp.max(scores, axis=1, keepdims=True)
                probs.append(jnp.exp(scores - top).astype(BF16))
                here = (lane % 8 == pair * 2 + side) & (lane < TOP_COLS)
                stat = jnp.where(here, top, stat)
            result = jnp.dot(
                jnp.concatenate(probs, axis=1), vaug[pair], preferred_element_type=F32
            )
            numer_out[:, cols] = result[:, :128].astype(numer_out.dtype)
            stat = stat + result[:, 128:]
        stat_out[...] = encode(stat)

    attend(
        pl.multiple_of((1 - c) * half, half), core_out.at[:, :width], core_out.at[:, width:]
    )
    pl.semaphore_wait(barrier, 1 + deep)
    sent = [copy(0, core_out, core_in, sibling)]
    sent[0].start()
    attend(pl.multiple_of(c * half, half), own_numer, own_stat)
    sent[0].wait_recv()

    def chip_sum(at):
        at = pl.multiple_of(at, quarter)
        return merge(
            [own_numer[pl.ds(at, quarter), :], core_in[pl.ds(at, quarter), :width]],
            [own_stat[pl.ds(at, quarter), :], core_in[pl.ds(at, quarter), width:]],
            spread,
            width,
        )

    order = list(range(1, deep)) + [0]
    index = 1
    x_copies = {}
    x_numer, x_stat = chip_sum((1 - x) * quarter)
    x_out[:, :width] = x_numer.astype(BF16)
    x_out[:, width:] = x_stat
    for k in order:
        block = pl.ds(pl.multiple_of(lax.rem(w + k, deep) * piece, piece), piece)
        x_copies[k] = copy(index, x_out.at[block], x_in.at[k], across)
        x_copies[k].start()
        index += 1
    x_numer, x_stat = chip_sum(x * quarter)
    mine_numer[...] = x_numer
    mine_stat[...] = x_stat
    mine = {}
    for k in order:
        block = pl.ds(pl.multiple_of(lax.rem(w + k, deep) * piece, piece), piece)
        mine[k] = (mine_numer[block, :], mine_stat[block, :])
    z_copies = {}
    for k in order:
        x_copies[k].wait_recv()
        numer, stat = merge(
            [mine[k][0], x_in[k, :, :width]], [mine[k][1], x_in[k, :, width:]], spread, width
        )
        if k:
            z_out[k, :, :width] = numer.astype(BF16)
            z_out[k, :, width:] = stat
            z_copies[k] = copy(index, z_out.at[k], z_in.at[k], along[k])
            z_copies[k].start()
            index += 1
    numers, stats = [numer], [stat]
    for k in order[:-1]:
        z_copies[k].wait_recv()
        numers.append(z_in[k, :, :width])
        stats.append(z_in[k, :, width:])
    attended = merge_ratio(numers, stats, spread, width).astype(BF16)

    def place(core, column, slab):
        return pl.ds(pl.multiple_of(core * half + column * quarter + slab * piece, piece), piece)

    own = place(c, x, w)
    loads.wait(6, 8)
    mixed = latents[own, :].astype(F32) + jnp.dot(
        attended, w_out[...], preferred_element_type=F32
    )
    center = mixed - jnp.mean(mixed, axis=1, keepdims=True)
    variance = jnp.mean(center * center, axis=1, keepdims=True)
    out[own, :] = (center * lax.rsqrt(variance + 1e-05) * out_gain[...]).astype(BF16)

    z_gather, x_gather, s_gather = {}, {}, {}

    def gather(store, key, at, device):
        nonlocal index
        store[key] = copy(index, out.at[at], out.at[at], device)
        store[key].start()
        index += 1

    for k in range(1, deep):
        gather(z_gather, k, own, along[k])
    gather(x_gather, 0, own, across)
    gather(s_gather, 0, own, sibling)

    def relay(k):
        x_gather[k].wait_recv()
        gather(s_gather, deep + k, place(c, 1 - x, lax.rem(w + deep - k, deep)), sibling)

    for k in range(1, deep):
        z_gather[k].wait_recv()
        came = place(c, x, lax.rem(w + deep - k, deep))
        gather(x_gather, k, came, across)
        gather(s_gather, k, came, sibling)
        if k > 1:
            relay(k - 2)
    relay(deep - 2)
    relay(deep - 1)
    for k in range(2 * deep):
        s_gather[k].wait_recv()
    for store in (x_copies, z_copies, z_gather, x_gather, s_gather):
        sent += list(store.values())
    for one in sent:
        one.wait_send()


def body(deep, field, w_embed, embed_bias, w_query, w_key, w_value, w_out, latents, out_gain):
    tokens = field.shape[0]
    rows, width = latents.shape
    half, piece = rows // 2, rows // 4 // deep
    wide = width + 128
    arguments = (
        field,
        w_embed,
        embed_bias.reshape(1, width),
        w_query,
        w_key,
        w_value,
        w_out,
        latents,
        out_gain.reshape(1, width),
    )
    copies = 1 + deep + (deep - 1) + (deep - 1) + deep + 2 * deep
    macs = tokens * width * width * 3 + rows * width * width + 2 * rows * tokens * width
    return pl.pallas_call(
        functools.partial(kernel, deep),
        out_shape=jax.ShapeDtypeStruct((rows, width), BF16),
        in_specs=[pl.BlockSpec(memory_space=pltpu.HBM)] * 9,
        out_specs=pl.BlockSpec(memory_space=pltpu.VMEM),
        scratch_shapes=[pltpu.VMEM(a.shape, a.dtype) for a in arguments]
        + [
            pltpu.VMEM((rows, width), BF16),
            pltpu.VMEM((width, tokens), BF16),
            pltpu.VMEM((HEADS // 2, 2 * tokens, 256), BF16),
            pltpu.VMEM((128, 2 * width + 256), BF16),
            pltpu.VMEM((half, width), F32),
            pltpu.VMEM((half, 128), BF16),
            pltpu.VMEM((half, wide), BF16),
            pltpu.VMEM((half, wide), BF16),
            pltpu.VMEM((rows // 4, wide), BF16),
            pltpu.VMEM((deep, piece, wide), BF16),
            pltpu.VMEM((deep, piece, wide), BF16),
            pltpu.VMEM((deep, piece, wide), BF16),
            pltpu.VMEM((rows // 4, width), F32),
            pltpu.VMEM((rows // 4, 128), BF16),
            pltpu.SemaphoreType.DMA((copies,)),
            pltpu.SemaphoreType.DMA((copies,)),
            pltpu.SemaphoreType.DMA((9,)),
        ],
        compiler_params=pltpu.CompilerParams(
            collective_id=0, has_side_effects=True, vmem_limit_bytes=40 * 2**20
        ),
        cost_estimate=pl.CostEstimate(
            flops=2 * macs, bytes_accessed=5 * 2**20, transcendentals=rows * tokens * HEADS
        ),
    )(*[pltpu.with_memory_space_constraint(a, pltpu.HBM) for a in arguments])


def solution(mesh):
    placed = (P(("group", "wide", "narrow"), None), P(), P(), P(), P(), P(), P(), P(), P())
    deep = mesh.shape["wide"]

    def pick(field, *rest):
        rows, width = rest[6].shape
        fits = mesh.shape["narrow"] == 4 and 2 <= deep <= 8 and rows % (64 * deep) == 0
        fits = fits and width == HEADS * 64 and field.shape[0] % 256 == 0
        return (functools.partial(body, deep) if fits else plain_body)(field, *rest)

    return jax.shard_map(
        pick, mesh=mesh, in_specs=placed, out_specs=P("group", None), check_vma=False
    )
```
